256 devices in a mesh: blk: 64 (over y_hi, z, x), grp: 4 (over y_lo, core).
Axes of the slice: x: 4, y: 4 (y_hi: 2, y_lo: 2; y = y_hi * 2 + y_lo), z: 8, core: 2. Of those that a mesh axis runs over, the one named last changes fastest.
Arguments:
- images: bfloat16 [65536, 1152], P(('blk', 'grp')), may hold values from -0.1875 to 0.1875
- captions: bfloat16 [65536, 1152], P(('blk', 'grp')), may hold values from -0.1875 to 0.1875
- labels: int32 [65536], P(('blk', 'grp')), may hold values from 0 to 65535, as said below
- log_scale: float32 [1], replicated, may hold values from 1.6 to 2.4
- logit_bias: float32 [1], replicated, may hold values from -3 to -1
Outputs:
- row_loss: float32 [65536], P(('blk', 'grp'))
- image_grad: float32 [65536, 1152], P(('blk', 'grp'))
- caption_grad: float32 [65536, 1152], P(('blk', 'grp'))
The draws below stay inside these ranges and needn't reach their ends.
Inputs may be any that keep to these rules, and one draw needn't show every extreme that they name: labels[i] lies in the same block of 1024 rows as i, and within each block the labels are a permutation of that block's rows.
All inputs are finite; a program needn't handle non-finite values.
Results may differ from the reference program's by a relative error of at most 0.0055.
Values may be sent and summed in bfloat16 or wider, within the bound.
A program may use at most 128 MiB of HBM per device.

```python
import jax
import jax.numpy as jnp
from jax import lax

D = 1152
STEPS = 3
BLOCK = 1024
BATCH = 65536


def draw_labels(key, part):
    key = jax.random.fold_in(key, 7)
    block_count = BATCH // BLOCK
    keys = jax.random.split(key, block_count)
    orders = jax.vmap(lambda single: jax.random.permutation(single, BLOCK))(keys)
    offsets = jnp.arange(block_count, dtype=jnp.int32)[:, None] * BLOCK
    return (orders.astype(jnp.int32) + offsets).reshape(BATCH).astype(jnp.int32)


def shard_levels(stream_key, extent, cuts, smallest, high):
    def one(position, parts):
        heights = jax.random.uniform(jax.random.fold_in(jax.random.fold_in(stream_key, 6), position), (parts,), jnp.float32, smallest / len(cuts), high / len(cuts))
        return jnp.repeat(jnp.exp(heights), extent[position] // parts).reshape((-1,) + (1,) * (len(extent) - position - 1))

    factor_of = one(*cuts[0])
    for cut in cuts[1:]:
        factor_of = factor_of * one(*cut)
    return factor_of


def scatter_about(rng, dims, scale, reach, cuts=(), kind=jnp.bfloat16):
    loudness = shard_levels(rng, dims, cuts, -0.22, 0.18) if cuts else 1.0
    array = jax.random.normal(rng, dims, jnp.float32) * scale * loudness
    return jnp.minimum(jnp.maximum(array, -reach), reach).astype(kind)


def setup_inputs(seed: int = 0) -> dict:
    streams_of = jax.random.split(jax.random.key(seed), 6)
    images = scatter_about(streams_of[0], (BATCH, D), (D ** -0.5), 0.1875, ((0, 256),))
    captions = scatter_about(streams_of[1], (BATCH, D), (D ** -0.5), 0.1875, ((0, 256),))
    labels = draw_labels(jax.random.fold_in(streams_of[5], 71), 0)
    log_scale = jnp.clip(jax.random.uniform(streams_of[3], (1,), jnp.float32, 1.6, 2.4), 1.6, 2.4)
    logit_bias = jnp.clip(jax.random.uniform(streams_of[4], (1,), jnp.float32, -3.0, -1.0), -3.0, -1.0)
    return dict(images=images, captions=captions, labels=labels, log_scale=log_scale, logit_bias=logit_bias)


epsilon = 1e-06

def normalize(values):
    widened = values.astype(jnp.float32)
    inverse = lax.rsqrt(lax.optimization_barrier(jnp.sum(widened * widened, -1, keepdims=True)) + epsilon)
    return (inverse, widened * inverse)

def unnormalize(inverse, unit_rows, pull):
    return inverse * (pull - unit_rows * lax.optimization_barrier(jnp.sum(unit_rows * pull, -1, keepdims=True)))

def reference(images, captions, labels, log_scale, logit_bias):
    inv_img, img_unit32 = normalize(images)
    inv_cap, cap_unit32 = normalize(captions)
    img_unit = img_unit32.astype(jnp.bfloat16)
    cap_unit = cap_unit32.astype(jnp.bfloat16)
    logit_scale = jnp.exp(log_scale[0])
    block_count = BATCH // BLOCK
    img_blocks = img_unit.reshape(block_count, BLOCK, D).astype(jnp.float32)
    cap_blocks = cap_unit.reshape(block_count, BLOCK, D).astype(jnp.float32)
    label_blocks = labels.reshape(block_count, BLOCK)
    columns = jnp.arange(BLOCK, dtype=jnp.int32)
    block_starts = jnp.arange(block_count, dtype=jnp.int32) * BLOCK
    img_pull = jnp.zeros((block_count, BLOCK, D), jnp.float32)
    cap_pull = jnp.zeros((block_count, BLOCK, D), jnp.float32)
    loss_sum = jnp.zeros((block_count, BLOCK), jnp.float32)
    for cycle_step in range(STEPS):
        visiting = jnp.roll(cap_blocks, cycle_step, axis=0)
        starts = jnp.roll(block_starts, cycle_step)
        logits = logit_scale * jnp.einsum('kid,kjd->kij', img_blocks, visiting) + logit_bias[0]
        positive = label_blocks[:, :, None] == starts[:, None, None] + columns[None, None, :]
        signs = jnp.where(positive, 1.0, -1.0).astype(jnp.float32)
        loss_sum = loss_sum + lax.optimization_barrier(jnp.sum(-jax.nn.log_sigmoid(signs * logits), -1))
        rounded = lax.optimization_barrier((jax.nn.sigmoid(logits) - positive.astype(jnp.float32)).astype(jnp.bfloat16))
        pair_weight = rounded.astype(jnp.float32)
        img_pull = img_pull + jnp.einsum('kij,kjd->kid', pair_weight, visiting)
        cap_pull = cap_pull + jnp.roll(jnp.einsum('kij,kid->kjd', pair_weight, img_blocks), -cycle_step, axis=0)
    img_pull = logit_scale * img_pull.reshape(BATCH, D)
    cap_pull = logit_scale * cap_pull.reshape(BATCH, D)
    row_loss = loss_sum.reshape(BATCH) / (STEPS * BLOCK)
    image_grad = unnormalize(inv_img, img_unit32, img_pull)
    caption_grad = unnormalize(inv_cap, cap_unit32, cap_pull)
    return (row_loss, image_grad, caption_grad)
```

```python
import jax
import jax.numpy as jnp
from jax import lax
from jax.sharding import PartitionSpec as P

STEPS = 3


epsilon = 1e-06


def passed_along(value, axis, steps):
    count = lax.axis_size(axis)
    pairs = [(source, (source + steps) % count) for source in range(count)]
    return lax.ppermute(value, axis, pairs)


def normalize(values):
    widened = values.astype(jnp.float32)
    inverse = lax.rsqrt(jnp.sum(widened * widened, -1, keepdims=True) + epsilon)
    return (inverse, widened * inverse)


def unnormalize(inverse, unit_rows, pull):
    return inverse * (pull - unit_rows * jnp.sum(unit_rows * pull, -1, keepdims=True))


def body(images, captions, labels, log_scale, logit_bias):
    row_count = images.shape[0]
    group_size = lax.axis_size("grp")
    cycle_index = lax.axis_index("blk")
    member = lax.axis_index("grp")
    block_rows = row_count * group_size
    logit_scale = jnp.exp(log_scale[0])
    inv_img, img_unit32 = normalize(images)
    inv_cap, cap_unit32 = normalize(captions)
    img_unit = img_unit32.astype(jnp.bfloat16)
    cap_unit = cap_unit32.astype(jnp.bfloat16)
    texts = [cap_unit, passed_along(cap_unit, "blk", 1), passed_along(cap_unit, "blk", 2)]
    all_images = lax.all_gather(img_unit, "grp", axis=0, tiled=True)
    all_labels = lax.all_gather(labels, "grp", axis=0, tiled=True)
    rows = lax.broadcasted_iota(jnp.int32, (row_count, 1), 0) + (cycle_index * block_rows + member * row_count)
    loss_sum = jnp.zeros((block_rows,), jnp.float32)
    img_pull = jnp.zeros((block_rows, images.shape[1]), jnp.float32)
    terms = []
    for step in range(STEPS):
        logits = (
            logit_scale
            * lax.dot_general(
                texts[step], all_images, (((1,), (1,)), ((), ())), preferred_element_type=jnp.float32
            )
            + logit_bias[0]
        )
        weight = jax.nn.sigmoid(logits)
        if step == 0:
            positive = all_labels[None, :] == rows
            loss_sum = loss_sum + jnp.sum(-jax.nn.log_sigmoid(jnp.where(positive, logits, -logits)), 0)
            weight = weight - positive.astype(jnp.float32)
        else:
            loss_sum = loss_sum + jnp.sum(-jax.nn.log_sigmoid(-logits), 0)
        weight = weight.astype(jnp.bfloat16)
        terms.append(jnp.dot(weight, all_images, preferred_element_type=jnp.float32))
        img_pull = img_pull + lax.dot_general(
            weight, texts[step], (((0,), (0,)), ((), ())), preferred_element_type=jnp.float32
        )
    cap_pull = terms[0]
    for step in range(1, STEPS):
        cap_pull = cap_pull + passed_along(terms[step].astype(jnp.bfloat16), "blk", -step).astype(jnp.float32)
    own_pull = lax.psum_scatter(img_pull.astype(jnp.bfloat16), "grp", scatter_dimension=0, tiled=True).astype(jnp.float32)
    row_loss = lax.psum_scatter(loss_sum, "grp", scatter_dimension=0, tiled=True) / (STEPS * block_rows)
    image_grad = unnormalize(inv_img, img_unit32, logit_scale * own_pull)
    caption_grad = unnormalize(inv_cap, cap_unit32, logit_scale * cap_pull)
    return (row_loss, image_grad, caption_grad)


def solution(mesh):
    in_specs = (P(("blk", "grp"), None), P(("blk", "grp"), None), P(("blk", "grp")), P(), P())
    out_specs = (P(("blk", "grp")), P(("blk", "grp"), None), P(("blk", "grp"), None))
    return jax.shard_map(body, mesh=mesh, in_specs=in_specs, out_specs=out_specs, check_vma=False)
```

```python
import functools

import jax
import jax.numpy as jnp
from jax import lax
from jax.experimental import pallas as pl
from jax.experimental.pallas import tpu as pltpu
from jax.sharding import PartitionSpec as P

STEPS = 3
CHUNK = 128
MIB = 2**20

epsilon = 1e-06

f32 = jnp.float32
bf16 = jnp.bfloat16


def places(axes):
    blk_size, _ = axes
    half = blk_size // 2
    blk = lax.axis_index("blk")
    grp = lax.axis_index("grp")
    chip, core = grp // 2, grp % 2

    def along(steps):
        other = (blk + steps + blk_size) % blk_size
        other_chip = (chip + blk // half + other // half) % 2
        return (other, other_chip * 2 + core)

    return dict(
        core=(blk, chip * 2 + 1 - core),
        pair=(blk, (1 - chip) * 2 + core),
        cross=(blk, (1 - chip) * 2 + 1 - core),
        next1=along(1),
        next2=along(2),
        last1=along(-1),
        last2=along(-2),
    )


def kernel(axes, log_scale_ref, bias_ref, img_ref, cap_ref, lab_ref, loss_ref, dimg_ref, dcap_ref,
           imgs, caps, weights, labs, inv_img, inv_cap, loss_acc, loss_in,
           back1, back2, in1, in2, core_out2, core_in2, core_out0, core_in0, pair_out, pair_in,
           send_sems, recv_sems):
    rows, width = img_ref.shape
    block_rows = 4 * rows
    count = rows // CHUNK
    place = places(axes)
    used = [0]
    started = []

    def copy(source, target, to):
        index = used[0]
        used[0] += 1
        made = pltpu.make_async_remote_copy(
            src_ref=source, dst_ref=target, send_sem=send_sems.at[index], recv_sem=recv_sems.at[index],
            device_id=place[to], device_id_type=pl.DeviceIdType.MESH)
        started.append(made)
        return made

    def chunk(index):
        return pl.ds(index * CHUNK, CHUNK)

    barrier = pltpu.get_barrier_semaphore()
    for to in place.values():
        pl.semaphore_signal(barrier, inc=1, device_id=to, device_id_type=pl.DeviceIdType.MESH)

    scale = jnp.exp(jnp.full((1, 1), log_scale_ref[0], f32))
    bias = bias_ref[0]

    def normalize(source, part, inverse_ref, target):
        wide = source[part, :].astype(f32)
        inverse = lax.rsqrt(jnp.sum(wide * wide, -1, keepdims=True) + epsilon)
        inverse_ref[part, :] = inverse
        target[part, :] = (wide * inverse).astype(bf16)

    for i in range(count):
        normalize(img_ref, chunk(i), inv_img, imgs)
    for i in range(count):
        normalize(cap_ref, chunk(i), inv_cap, caps)

    pl.semaphore_wait(barrier, len(place))

    lab_copies = [copy(lab_ref, labs.at[slot], to) for slot, to in ((1, "core"), (2, "pair"), (3, "cross"))]
    to_core = copy(imgs.at[pl.ds(0, rows)], imgs.at[pl.ds(rows, rows)], "core")
    to_pair = [copy(imgs.at[chunk(i)], imgs.at[pl.ds(2 * rows + i * CHUNK, CHUNK)], "pair") for i in range(count)]
    relays = [copy(imgs.at[pl.ds(2 * rows + i * CHUNK, CHUNK)], imgs.at[pl.ds(3 * rows + i * CHUNK, CHUNK)], "core")
              for i in range(count)]
    ahead = {}
    for i in range(count):
        for step, to in ((2, "next2"), (1, "next1")):
            ahead[step, i] = copy(caps.at[chunk(i)], caps.at[pl.ds(step * rows + i * CHUNK, CHUNK)], to)
    for made in lab_copies:
        made.start()
    to_core.start()
    for i in range(count):
        to_pair[i].start()
        ahead[2, i].start()
        ahead[1, i].start()
    labs[0] = lab_ref[...]

    row_index = lax.broadcasted_iota(jnp.int32, (rows, 1), 0) + (
        lax.axis_index("blk") * block_rows + lax.axis_index("grp") * rows)

    def score(start, size, slot, diagonal=False):
        dots = lax.dot_general(caps[pl.ds(start, size), :], imgs[pl.ds(slot * rows, rows), :],
                               (((1,), (1,)), ((), ())), preferred_element_type=f32)
        logits = scale * dots + bias
        grown = jnp.exp(logits)
        total = 1.0 + grown
        inverse = 1.0 / total
        loss = jnp.log(total) + (grown - (total - 1.0)) * inverse
        weight = grown * inverse
        if diagonal:
            positive = labs[slot] == row_index
            loss = loss - jnp.where(positive, logits, 0.0)
            weight = weight - jnp.where(positive, 1.0, 0.0)
        weights[pl.ds(start, size), pl.ds(slot * rows, rows)] = weight.astype(bf16)
        part = jnp.sum(loss, 0, keepdims=True)
        loss_acc[slot] = part if diagonal else loss_acc[slot] + part

    for made in lab_copies:
        made.wait_recv()
    score(0, rows, 0, True)
    to_core.wait_recv()
    score(0, rows, 1, True)
    for i in range(count):
        to_pair[i].wait_recv()
        relays[i].start()
    score(0, rows, 2, True)
    for i in range(count):
        relays[i].wait_recv()
    score(0, rows, 3, True)

    returns = {}
    for i in range(count):
        for step, to, out, landing in ((2, "last2", back2, in2), (1, "last1", back1, in1)):
            ahead[step, i].wait_recv()
            start = step * rows + i * CHUNK
            for slot in range(4):
                score(start, CHUNK, slot)
            out[chunk(i), :] = jnp.dot(weights[pl.ds(start, CHUNK), :], imgs[...],
                                       preferred_element_type=f32).astype(bf16)
            returns[step, i] = copy(out.at[chunk(i)], landing.at[chunk(i)], to)
            returns[step, i].start()

    loss_copies = [copy(loss_acc.at[slot], loss_in.at[slot - 1], to)
                   for slot, to in ((1, "core"), (2, "pair"), (3, "cross"))]
    for made in loss_copies:
        made.start()

    def image_terms(slot, i):
        return lax.dot_general(weights[:, pl.ds(slot * rows + i * CHUNK, CHUNK)], caps[...],
                               (((0,), (0,)), ((), ())), preferred_element_type=f32)

    core2, core0, pairs = [], [], []
    for i in range(count):
        core_out2[chunk(i), :] = image_terms(3, i).astype(bf16)
        core2.append(copy(core_out2.at[chunk(i)], core_in2.at[chunk(i)], "core"))
        core2[i].start()
    for i in range(count):
        own = image_terms(2, i)
        core2[i].wait_recv()
        pair_out[chunk(i), :] = (own + core_in2[chunk(i), :].astype(f32)).astype(bf16)
        pairs.append(copy(pair_out.at[chunk(i)], pair_in.at[chunk(i)], "pair"))
        pairs[i].start()
    for i in range(count):
        core_out0[chunk(i), :] = image_terms(1, i).astype(bf16)
        core0.append(copy(core_out0.at[chunk(i)], core_in0.at[chunk(i)], "core"))
        core0[i].start()
    for i in range(count):
        dimg_ref[chunk(i), :] = image_terms(0, i)
    for i in range(count):
        dcap_ref[chunk(i), :] = jnp.dot(weights[chunk(i), :], imgs[...], preferred_element_type=f32)
    for i in range(count):
        core0[i].wait_recv()
        dimg_ref[chunk(i), :] = dimg_ref[chunk(i), :] + core_in0[chunk(i), :].astype(f32)

    for made in loss_copies:
        made.wait_recv()
    loss_ref[...] = (loss_acc[0] + loss_in[0] + loss_in[1] + loss_in[2]) / (STEPS * block_rows)

    def unnormalize(source, part, inverse_ref, pull):
        inverse = inverse_ref[part, :]
        unit = source[part, :].astype(f32) * inverse
        pull = scale * pull
        return inverse * (pull - unit * jnp.sum(unit * pull, -1, keepdims=True))

    for i in range(count):
        returns[2, i].wait_recv()
        returns[1, i].wait_recv()
        pull = dcap_ref[chunk(i), :] + in1[chunk(i), :].astype(f32) + in2[chunk(i), :].astype(f32)
        dcap_ref[chunk(i), :] = unnormalize(cap_ref, chunk(i), inv_cap, pull)
    for i in range(count):
        pairs[i].wait_recv()
        pull = dimg_ref[chunk(i), :] + pair_in[chunk(i), :].astype(f32)
        dimg_ref[chunk(i), :] = unnormalize(img_ref, chunk(i), inv_img, pull)
    for made in started:
        made.wait_send()


def body(axes, images, captions, labels, log_scale, logit_bias):
    rows, width = images.shape
    vmem = pl.BlockSpec(memory_space=pltpu.VMEM)
    smem = pl.BlockSpec(memory_space=pltpu.SMEM)
    own = pltpu.VMEM((rows, width), bf16)
    loss, image_grad, caption_grad = pl.pallas_call(
        functools.partial(kernel, axes),
        out_shape=(
            jax.ShapeDtypeStruct((1, rows), f32),
            jax.ShapeDtypeStruct((rows, width), f32),
            jax.ShapeDtypeStruct((rows, width), f32),
        ),
        in_specs=[smem, smem, vmem, vmem, vmem],
        out_specs=(vmem, vmem, vmem),
        scratch_shapes=[
            pltpu.VMEM((4 * rows, width), bf16),
            pltpu.VMEM((STEPS * rows, width), bf16),
            pltpu.VMEM((STEPS * rows, 4 * rows), bf16),
            pltpu.VMEM((4, 1, rows), jnp.int32),
            pltpu.VMEM((rows, 1), f32),
            pltpu.VMEM((rows, 1), f32),
            pltpu.VMEM((4, 1, rows), f32),
            pltpu.VMEM((3, 1, rows), f32),
            own, own, own, own, own, own, own, own, own, own,
            pltpu.SemaphoreType.DMA((40,)),
            pltpu.SemaphoreType.DMA((40,)),
        ],
        compiler_params=pltpu.CompilerParams(
            collective_id=0, has_side_effects=True, vmem_limit_bytes=44 * MIB),
        cost_estimate=pl.CostEstimate(
            flops=2 * 3 * STEPS * rows * 4 * rows * width, bytes_accessed=12 * rows * width,
            transcendentals=2 * STEPS * rows * 4 * rows),
        name="contrast",
    )(log_scale, logit_bias, images, captions, labels.reshape(1, rows))
    return (loss.reshape(rows), image_grad, caption_grad)


def solution(mesh):
    axes = (mesh.shape["blk"], mesh.shape["grp"])
    in_specs = (P(("blk", "grp"), None), P(("blk", "grp"), None), P(("blk", "grp")), P(), P())
    out_specs = (P(("blk", "grp")), P(("blk", "grp"), None), P(("blk", "grp"), None))
    return jax.shard_map(functools.partial(body, axes), mesh=mesh, in_specs=in_specs, out_specs=out_specs, check_vma=False)
```

```python
import jax
import jax.numpy as jnp
from jax import lax
from jax.experimental import pallas as pl
from jax.experimental.pallas import tpu as pltpu
from jax.sharding import PartitionSpec as P

STEPS = 3
ROW = 4
MIB = 2**20

epsilon = 1e-06

f32 = jnp.float32
bf16 = jnp.bfloat16


def places():
    blk_size = lax.axis_size("blk")
    half = blk_size // 2
    blk = lax.axis_index("blk")
    grp = lax.axis_index("grp")
    chip, core = grp // 2, grp % 2

    def along(start, steps):
        other = (start + steps + blk_size) % blk_size
        other_chip = (chip + start // half + other // half) % 2
        return (other, other_chip * 2 + core)

    def beside(start, steps):
        return start - start % ROW + (start + steps + ROW) % ROW

    def source(steps, sideways):
        other, member = along(blk, steps)
        return (beside(other, sideways), member)

    targets = dict(
        core=(blk, chip * 2 + 1 - core),
        pair=(blk, (1 - chip) * 2 + core),
        cross=(blk, (1 - chip) * 2 + 1 - core),
        next=along(blk, 1),
        last=along(blk, -1),
        right=(beside(blk, 1), grp),
        left=(beside(blk, -1), grp),
        on=along(beside(blk, 1), 2),
        home=along(beside(blk, -1), -2),
    )
    sources = [targets[name] for name in ("core", "pair", "cross", "next", "last", "right", "left")]
    sources += [source(-2, -1), source(2, 1)]
    return targets, sources


def kernel(log_scale_ref, bias_ref, img_ref, cap_ref, lab_ref, loss_ref, dimg_ref, dcap_ref,
           imgs, caps, weights, labs, inv_img, inv_cap, loss_acc, loss_in, passing, own_terms,
           out_last, out_acc, out_far, acc_out, in_last, in_acc, in_passing, in_home, in_sum,
           core_out2, core_in2, core_out0, core_in0, pair_out, pair_in, send_sems, recv_sems):
    rows, width = img_ref.shape
    block_rows = 4 * rows
    piece, part = rows // 4, rows // 2
    place, sources = places()
    started = []

    def copy(source, target, to):
        index = len(started)
        made = pltpu.make_async_remote_copy(
            src_ref=source, dst_ref=target, send_sem=send_sems.at[index], recv_sem=recv_sems.at[index],
            device_id=place[to], device_id_type=pl.DeviceIdType.MESH)
        started.append(made)
        return made

    barrier = pltpu.get_barrier_semaphore()
    for to in sources:
        pl.semaphore_signal(barrier, inc=1, device_id=to, device_id_type=pl.DeviceIdType.MESH)

    scale = jnp.exp(jnp.full((1, 1), log_scale_ref[0], f32))
    bias = bias_ref[0]

    def normalize(source, span, inverse_ref, target):
        wide = source[span, :].astype(f32)
        inverse = lax.rsqrt(jnp.sum(wide * wide, -1, keepdims=True) + epsilon)
        inverse_ref[span, :] = inverse
        target[span, :] = (wide * inverse).astype(bf16)

    for i in range(2):
        normalize(img_ref, pl.ds(i * part, part), inv_img, imgs)
    for i in range(2):
        normalize(cap_ref, pl.ds(i * part, part), inv_cap, caps)

    pl.semaphore_wait(barrier, len(place))

    def at(ref, start, index, size=piece):
        return ref.at[pl.ds(start + index * size, size)]

    lab_copies = [copy(lab_ref, labs.at[slot], to) for slot, to in ((1, "core"), (2, "pair"), (3, "cross"))]
    to_core = copy(at(imgs, 0, 0, rows), at(imgs, rows, 0, rows), "core")
    to_pair = [copy(at(imgs, 0, i), at(imgs, 2 * rows, i), "pair") for i in range(4)]
    pair_on = [copy(at(imgs, 2 * rows, i), at(imgs, 3 * rows, i), "core") for i in range(4)]
    to_next = [copy(at(caps, 0, i), at(caps, rows, i), "next") for i in range(4)]
    next_on = [copy(at(caps, rows, i), at(caps, 2 * rows, i), "next") for i in range(2)]
    to_left = [copy(at(caps, part, i), at(passing, 0, i), "left") for i in range(2)]
    left_on = [copy(at(passing, 0, i), at(caps, 2 * rows + part, i), "on") for i in range(2)]

    for made in lab_copies:
        made.start()
    to_core.start()
    for i in range(4):
        to_pair[i].start()
        to_next[i].start()
        if i < 2:
            to_left[i].start()
    labs[0] = lab_ref[...]

    row_index = lax.broadcasted_iota(jnp.int32, (rows, 1), 0) + (
        lax.axis_index("blk") * block_rows + lax.axis_index("grp") * rows)
    for slot in range(4):
        loss_acc[slot] = jnp.zeros((1, rows), f32)

    def score(start, size, slot):
        dots = lax.dot_general(caps[pl.ds(start, size), :], imgs[pl.ds(slot * rows, rows), :],
                               (((1,), (1,)), ((), ())), preferred_element_type=f32)
        logits = scale * dots + bias
        grown = jnp.exp(logits)
        total = 1.0 + grown
        inverse = 1.0 / total
        loss = jnp.log(total) + (grown - (total - 1.0)) * inverse
        weight = grown * inverse
        if start < rows:
            positive = labs[slot] == row_index[start:start + size]
            loss = loss - jnp.where(positive, logits, 0.0)
            weight = weight - jnp.where(positive, 1.0, 0.0)
        weights[pl.ds(start, size), pl.ds(slot * rows, rows)] = weight.astype(bf16)
        loss_acc[slot] = loss_acc[slot] + jnp.sum(loss, 0, keepdims=True)

    def caption_terms(start, size):
        return jnp.dot(weights[pl.ds(start, size), :], imgs[...], preferred_element_type=f32)

    def image_terms(slot, i):
        return lax.dot_general(weights[:, pl.ds(slot * rows + i * part, part)], caps[...],
                               (((0,), (0,)), ((), ())), preferred_element_type=f32)

    for made in lab_copies:
        made.wait_recv()
    score(0, rows, 0)
    to_core.wait_recv()
    for i in range(4):
        to_next[i].wait_recv()
        if i < 2:
            next_on[i].start()
            to_left[i].wait_recv()
            left_on[i].start()
        to_pair[i].wait_recv()
        pair_on[i].start()
        if i == 0:
            score(0, rows, 1)
        if i == 1:
            score(rows, part, 0)
            score(rows, part, 1)
        if i == 2:
            left_on[0].wait_recv()
            left_on[1].wait_recv()
            score(2 * rows + part, part, 0)
            score(2 * rows + part, part, 1)
    score(rows + part, part, 0)
    score(rows + part, part, 1)
    score(rows + part, part, 2)
    score(2 * rows + part, part, 2)
    for i in range(4):
        pair_on[i].wait_recv()
    score(rows + part, part, 3)

    out_last[...] = caption_terms(rows + part, part).astype(bf16)
    to_last = copy(out_last, in_last, "last")
    to_last.start()
    score(2 * rows + part, part, 3)
    out_far[...] = caption_terms(2 * rows + part, part).astype(bf16)
    to_right = [copy(at(out_far, 0, i), at(in_passing, 0, i), "right") for i in range(2)]
    right_on = [copy(at(in_passing, 0, i), at(in_home, 0, i), "home") for i in range(2)]
    for made in to_right:
        made.start()
    score(rows, part, 2)
    score(rows, part, 3)
    own_terms[...] = caption_terms(rows, part)
    back = [copy(at(out_acc, 0, i), at(in_acc, 0, i), "last") for i in range(2)]
    for i in range(2):
        next_on[i].wait_recv()
        start = 2 * rows + i * piece
        for slot in range(4):
            score(start, piece, slot)
        out_acc[pl.ds(i * piece, piece), :] = caption_terms(start, piece).astype(bf16)
        back[i].start()
        if i == 0:
            score(0, rows, 2)
            score(0, rows, 3)

    core2 = [copy(at(core_out2, 0, i, part), at(core_in2, 0, i, part), "core") for i in range(2)]
    pairs = [copy(at(pair_out, 0, i, part), at(pair_in, 0, i, part), "pair") for i in range(2)]
    core0 = [copy(at(core_out0, 0, i, part), at(core_in0, 0, i, part), "core") for i in range(2)]
    sums = [copy(at(acc_out, 0, i), at(in_sum, 0, i), "last") for i in range(2)]
    loss_copies = [copy(loss_acc.at[slot], loss_in.at[slot - 1], to)
                   for slot, to in ((1, "core"), (2, "pair"), (3, "cross"))]
    for i in range(2):
        core_out2[pl.ds(i * part, part), :] = image_terms(3, i).astype(bf16)
        core2[i].start()
        own = image_terms(2, i)
        core2[i].wait_recv()
        pair_out[pl.ds(i * part, part), :] = (own + core_in2[pl.ds(i * part, part), :].astype(f32)).astype(bf16)
        pairs[i].start()
        to_right[i].wait_recv()
        right_on[i].start()
    for made in loss_copies:
        made.start()
    for i in range(2):
        back[i].wait_recv()
        span = pl.ds(i * piece, piece)
        acc_out[span, :] = (own_terms[span, :] + in_acc[span, :].astype(f32)).astype(bf16)
        sums[i].start()
        core_out0[pl.ds(i * part, part), :] = image_terms(1, i).astype(bf16)
        core0[i].start()
    for i in range(2):
        dimg_ref[pl.ds(i * part, part), :] = image_terms(0, i)
    for i in range(2):
        dcap_ref[pl.ds(i * part, part), :] = caption_terms(i * part, part)
    for i in range(2):
        core0[i].wait_recv()
        span = pl.ds(i * part, part)
        dimg_ref[span, :] = dimg_ref[span, :] + core_in0[span, :].astype(f32)

    for made in loss_copies:
        made.wait_recv()
    loss_ref[...] = (loss_acc[0] + loss_in[0] + loss_in[1] + loss_in[2]) / (STEPS * block_rows)

    def unnormalize(source, span, inverse_ref, pull):
        inverse = inverse_ref[span, :]
        unit = source[span, :].astype(f32) * inverse
        pull = scale * pull
        return inverse * (pull - unit * jnp.sum(unit * pull, -1, keepdims=True))

    to_last.wait_recv()
    for i in range(2):
        right_on[i].wait_recv()
        span, near = pl.ds(part + i * piece, piece), pl.ds(i * piece, piece)
        pull = dcap_ref[span, :] + in_last[near, :].astype(f32) + in_home[near, :].astype(f32)
        dcap_ref[span, :] = unnormalize(cap_ref, span, inv_cap, pull)
    for i in range(2):
        sums[i].wait_recv()
        span = pl.ds(i * piece, piece)
        pull = dcap_ref[span, :] + in_sum[span, :].astype(f32)
        dcap_ref[span, :] = unnormalize(cap_ref, span, inv_cap, pull)
    for i in range(2):
        pairs[i].wait_recv()
        span = pl.ds(i * part, part)
        pull = dimg_ref[span, :] + pair_in[span, :].astype(f32)
        dimg_ref[span, :] = unnormalize(img_ref, span, inv_img, pull)
    for made in started:
        made.wait_send()


def body(images, captions, labels, log_scale, logit_bias):
    rows, width = images.shape
    vmem = pl.BlockSpec(memory_space=pltpu.VMEM)
    smem = pl.BlockSpec(memory_space=pltpu.SMEM)
    own = pltpu.VMEM((rows, width), bf16)
    half = pltpu.VMEM((rows // 2, width), bf16)
    loss, image_grad, caption_grad = pl.pallas_call(
        kernel,
        out_shape=(
            jax.ShapeDtypeStruct((1, rows), f32),
            jax.ShapeDtypeStruct((rows, width), f32),
            jax.ShapeDtypeStruct((rows, width), f32),
        ),
        in_specs=[smem, smem, vmem, vmem, vmem],
        out_specs=(vmem, vmem, vmem),
        scratch_shapes=[
            pltpu.VMEM((4 * rows, width), bf16),
            pltpu.VMEM((STEPS * rows, width), bf16),
            pltpu.VMEM((STEPS * rows, 4 * rows), bf16),
            pltpu.VMEM((4, 1, rows), jnp.int32),
            pltpu.VMEM((rows, 1), f32),
            pltpu.VMEM((rows, 1), f32),
            pltpu.VMEM((4, 1, rows), f32),
            pltpu.VMEM((3, 1, rows), f32),
            half, pltpu.VMEM((rows // 2, width), f32),
            half, half, half, half, half, half, half, half, half,
            own, own, own, own, own, own,
            pltpu.SemaphoreType.DMA((40,)),
            pltpu.SemaphoreType.DMA((40,)),
        ],
        compiler_params=pltpu.CompilerParams(
            collective_id=0, has_side_effects=True, vmem_limit_bytes=44 * MIB),
        cost_estimate=pl.CostEstimate(
            flops=2 * 3 * STEPS * rows * 4 * rows * width, bytes_accessed=12 * rows * width,
            transcendentals=2 * STEPS * rows * 4 * rows),
        name="contrast",
    )(log_scale, logit_bias, images, captions, labels.reshape(1, rows))
    return (loss.reshape(rows), image_grad, caption_grad)


def solution(mesh):
    in_specs = (P(("blk", "grp"), None), P(("blk", "grp"), None), P(("blk", "grp")), P(), P())
    out_specs = (P(("blk", "grp")), P(("blk", "grp"), None), P(("blk", "grp"), None))
    return jax.shard_map(body, mesh=mesh, in_specs=in_specs, out_specs=out_specs, check_vma=False)
```

```python
import jax
import jax.numpy as jnp
from jax import lax
from jax.experimental import pallas as pl
from jax.experimental.pallas import tpu as pltpu
from jax.sharding import PartitionSpec as P

STEPS = 3
ROW = 4
MIB = 2**20

epsilon = 1e-06

f32 = jnp.float32
bf16 = jnp.bfloat16


def places():
    blk_size = lax.axis_size("blk")
    half = blk_size // 2
    blk = lax.axis_index("blk")
    grp = lax.axis_index("grp")
    chip, core = grp // 2, grp % 2

    def along(start, steps):
        other = (start + steps + blk_size) % blk_size
        other_chip = (chip + start // half + other // half) % 2
        return (other, other_chip * 2 + core)

    def beside(start, steps):
        return start - start % ROW + (start + steps + ROW) % ROW

    def crosses(start, steps):
        return (start // half + (start + steps + blk_size) % blk_size // half) % 2

    def side(start, steps):
        change = crosses(start, 2 * steps)
        return (beside(start, -steps) + change * half) % blk_size, change

    def served(start, steps):
        other = beside(start, steps)
        change = crosses(other, 2 * steps)
        return (other + change * half) % blk_size, change

    def member(change):
        return (chip + change) % 2 * 2 + core

    left, left_change = side(blk, 1)
    right, right_change = side(blk, -1)
    from_right, from_right_change = served(blk, 1)
    from_left, from_left_change = served(blk, -1)
    targets = dict(
        core=(blk, chip * 2 + 1 - core),
        pair=(blk, (1 - chip) * 2 + core),
        cross=(blk, (1 - chip) * 2 + 1 - core),
        next=along(blk, 1),
        last=along(blk, -1),
        left=(left, member(left_change)),
        right=(right, member(right_change)),
        on=((from_right + 2) % blk_size, grp),
        home=((from_left - 2 + blk_size) % blk_size, grp),
    )
    sources = [targets[name] for name in ("core", "pair", "cross", "next", "last")]
    sources += [(from_right, member(from_right_change)), (from_left, member(from_left_change))]
    sources += [(side((blk - 2 + blk_size) % blk_size, 1)[0], grp), (side((blk + 2) % blk_size, -1)[0], grp)]
    return targets, sources


def kernel(log_scale_ref, bias_ref, img_hbm, cap_hbm, lab_hbm, loss_ref, dimg_ref, dcap_ref,
           img_ref, cap_ref, lab_ref, load_sems, imgs, caps, weights, labs, inv_img, inv_cap, loss_acc, loss_in, passing, own_terms,
           out_last, out_acc, out_far, acc_out, in_last, in_acc, in_passing, in_home, in_sum,
           core_out2, core_in2, core_out0, core_in0, pair_out, pair_in, send_sems, recv_sems):
    rows, width = dimg_ref.shape
    block_rows = 4 * rows
    piece, part = rows // 4, rows // 2
    place, sources = places()
    started = []

    def copy(source, target, to):
        index = len(started)
        made = pltpu.make_async_remote_copy(
            src_ref=source, dst_ref=target, send_sem=send_sems.at[index], recv_sem=recv_sems.at[index],
            device_id=place[to], device_id_type=pl.DeviceIdType.MESH)
        started.append(made)
        return made

    barrier = pltpu.get_barrier_semaphore()
    for to in sources:
        pl.semaphore_signal(barrier, inc=1, device_id=to, device_id_type=pl.DeviceIdType.MESH)

    loads = [pltpu.make_async_copy(source, target, load_sems.at[i])
             for i, (source, target) in enumerate(((img_hbm, img_ref), (cap_hbm, cap_ref), (lab_hbm, lab_ref)))]
    for made in loads:
        made.start()
    scale = jnp.exp(jnp.full((1, 1), log_scale_ref[0], f32))
    bias = bias_ref[0]

    def normalize(source, span, inverse_ref, target):
        wide = source[span, :].astype(f32)
        inverse = lax.rsqrt(jnp.sum(wide * wide, -1, keepdims=True) + epsilon)
        inverse_ref[span, :] = inverse
        target[span, :] = (wide * inverse).astype(bf16)

    loads[0].wait()
    for i in range(2):
        normalize(img_ref, pl.ds(i * part, part), inv_img, imgs)
    loads[1].wait()
    for i in range(2):
        normalize(cap_ref, pl.ds(i * part, part), inv_cap, caps)

    loads[2].wait()
    pl.semaphore_wait(barrier, len(place))

    def at(ref, start, index, size=piece):
        return ref.at[pl.ds(start + index * size, size)]

    lab_copies = [copy(lab_ref, labs.at[slot], to) for slot, to in ((1, "core"), (2, "pair"), (3, "cross"))]
    to_core = copy(at(imgs, 0, 0, rows), at(imgs, rows, 0, rows), "core")
    to_pair = [copy(at(imgs, 0, i), at(imgs, 2 * rows, i), "pair") for i in range(4)]
    pair_on = [copy(at(imgs, 2 * rows, i), at(imgs, 3 * rows, i), "core") for i in range(4)]
    to_next = [copy(at(caps, 0, i), at(caps, rows, i), "next") for i in range(4)]
    next_on = [copy(at(caps, rows, i), at(caps, 2 * rows, i), "next") for i in range(2)]
    to_left = [copy(at(caps, part, i), at(passing, 0, i), "left") for i in range(2)]
    left_on = [copy(at(passing, 0, i), at(caps, 2 * rows + part, i), "on") for i in range(2)]

    for made in lab_copies:
        made.start()
    to_core.start()
    for i in range(4):
        to_pair[i].start()
        to_next[i].start()
        if i < 2:
            to_left[i].start()
    labs[0] = lab_ref[...]

    row_index = lax.broadcasted_iota(jnp.int32, (rows, 1), 0) + (
        lax.axis_index("blk") * block_rows + lax.axis_index("grp") * rows)
    for slot in range(4):
        loss_acc[slot] = jnp.zeros((1, rows), f32)

    def score(start, size, slot):
        dots = lax.dot_general(caps[pl.ds(start, size), :], imgs[pl.ds(slot * rows, rows), :],
                               (((1,), (1,)), ((), ())), preferred_element_type=f32)
        logits = scale * dots + bias
        grown = jnp.exp(logits)
        total = 1.0 + grown
        inverse = 1.0 / total
        loss = jnp.log(total) + (grown - (total - 1.0)) * inverse
        weight = grown * inverse
        if start < rows:
            positive = labs[slot] == row_index[start:start + size]
            loss = loss - jnp.where(positive, logits, 0.0)
            weight = weight - jnp.where(positive, 1.0, 0.0)
        weights[pl.ds(start, size), pl.ds(slot * rows, rows)] = weight.astype(bf16)
        loss_acc[slot] = loss_acc[slot] + jnp.sum(loss, 0, keepdims=True)

    def caption_terms(start, size):
        return jnp.dot(weights[pl.ds(start, size), :], imgs[...], preferred_element_type=f32)

    def image_terms(slot, i):
        return lax.dot_general(weights[:, pl.ds(slot * rows + i * part, part)], caps[...],
                               (((0,), (0,)), ((), ())), preferred_element_type=f32)

    for made in lab_copies:
        made.wait_recv()
    score(0, rows, 0)
    to_core.wait_recv()
    for i in range(4):
        to_next[i].wait_recv()
        if i < 2:
            next_on[i].start()
            to_left[i].wait_recv()
            left_on[i].start()
        to_pair[i].wait_recv()
        pair_on[i].start()
        if i == 0:
            score(0, rows, 1)
        if i == 1:
            score(rows, part, 0)
            score(rows, part, 1)
        if i == 2:
            left_on[0].wait_recv()
            left_on[1].wait_recv()
            score(2 * rows + part, part, 0)
            score(2 * rows + part, part, 1)
    score(rows + part, part, 0)
    score(rows + part, part, 1)
    score(rows + part, part, 2)
    score(2 * rows + part, part, 2)
    for i in range(4):
        pair_on[i].wait_recv()
    score(rows + part, part, 3)

    out_last[...] = caption_terms(rows + part, part).astype(bf16)
    to_last = copy(out_last, in_last, "last")
    to_last.start()
    score(2 * rows + part, part, 3)
    out_far[...] = caption_terms(2 * rows + part, part).astype(bf16)
    to_right = [copy(at(out_far, 0, i), at(in_passing, 0, i), "right") for i in range(2)]
    right_on = [copy(at(in_passing, 0, i), at(in_home, 0, i), "home") for i in range(2)]
    for made in to_right:
        made.start()
    score(rows, part, 2)
    score(rows, part, 3)
    own_terms[...] = caption_terms(rows, part)
    back = [copy(at(out_acc, 0, i), at(in_acc, 0, i), "last") for i in range(2)]
    for i in range(2):
        next_on[i].wait_recv()
        start = 2 * rows + i * piece
        for slot in range(4):
            score(start, piece, slot)
        out_acc[pl.ds(i * piece, piece), :] = caption_terms(start, piece).astype(bf16)
        back[i].start()
        if i == 0:
            score(0, rows, 2)
            score(0, rows, 3)

    core2 = [copy(at(core_out2, 0, i, part), at(core_in2, 0, i, part), "core") for i in range(2)]
    pairs = [copy(at(pair_out, 0, i, part), at(pair_in, 0, i, part), "pair") for i in range(2)]
    core0 = [copy(at(core_out0, 0, i, part), at(core_in0, 0, i, part), "core") for i in range(2)]
    sums = [copy(at(acc_out, 0, i), at(in_sum, 0, i), "last") for i in range(2)]
    loss_copies = [copy(loss_acc.at[slot], loss_in.at[slot - 1], to)
                   for slot, to in ((1, "core"), (2, "pair"), (3, "cross"))]
    for i in range(2):
        core_out2[pl.ds(i * part, part), :] = image_terms(3, i).astype(bf16)
        core2[i].start()
        own = image_terms(2, i)
        core2[i].wait_recv()
        pair_out[pl.ds(i * part, part), :] = (own + core_in2[pl.ds(i * part, part), :].astype(f32)).astype(bf16)
        pairs[i].start()
        to_right[i].wait_recv()
        right_on[i].start()
    for made in loss_copies:
        made.start()
    for i in range(2):
        back[i].wait_recv()
        span = pl.ds(i * piece, piece)
        acc_out[span, :] = (own_terms[span, :] + in_acc[span, :].astype(f32)).astype(bf16)
        sums[i].start()
        core_out0[pl.ds(i * part, part), :] = image_terms(1, i).astype(bf16)
        core0[i].start()
    for i in range(2):
        dimg_ref[pl.ds(i * part, part), :] = image_terms(0, i)
    for i in range(2):
        dcap_ref[pl.ds(i * part, part), :] = caption_terms(i * part, part)
    for i in range(2):
        core0[i].wait_recv()
        span = pl.ds(i * part, part)
        dimg_ref[span, :] = dimg_ref[span, :] + core_in0[span, :].astype(f32)

    for made in loss_copies:
        made.wait_recv()
    loss_ref[...] = (loss_acc[0] + loss_in[0] + loss_in[1] + loss_in[2]) / (STEPS * block_rows)

    def unnormalize(source, span, inverse_ref, pull):
        inverse = inverse_ref[span, :]
        unit = source[span, :].astype(f32) * inverse
        pull = scale * pull
        return inverse * (pull - unit * jnp.sum(unit * pull, -1, keepdims=True))

    to_last.wait_recv()
    for i in range(2):
        right_on[i].wait_recv()
        span, near = pl.ds(part + i * piece, piece), pl.ds(i * piece, piece)
        pull = dcap_ref[span, :] + in_last[near, :].astype(f32) + in_home[near, :].astype(f32)
        dcap_ref[span, :] = unnormalize(cap_ref, span, inv_cap, pull)
    for i in range(2):
        sums[i].wait_recv()
        span = pl.ds(i * piece, piece)
        pull = dcap_ref[span, :] + in_sum[span, :].astype(f32)
        dcap_ref[span, :] = unnormalize(cap_ref, span, inv_cap, pull)
    for i in range(2):
        pairs[i].wait_recv()
        span = pl.ds(i * part, part)
        pull = dimg_ref[span, :] + pair_in[span, :].astype(f32)
        dimg_ref[span, :] = unnormalize(img_ref, span, inv_img, pull)
    for made in started:
        made.wait_send()


def body(images, captions, labels, log_scale, logit_bias):
    rows, width = images.shape
    vmem = pl.BlockSpec(memory_space=pltpu.VMEM)
    hbm = pl.BlockSpec(memory_space=pltpu.HBM)
    smem = pl.BlockSpec(memory_space=pltpu.SMEM)
    own = pltpu.VMEM((rows, width), bf16)
    half = pltpu.VMEM((rows // 2, width), bf16)
    loss, image_grad, caption_grad = pl.pallas_call(
        kernel,
        out_shape=(
            jax.ShapeDtypeStruct((1, rows), f32),
            jax.ShapeDtypeStruct((rows, width), f32),
            jax.ShapeDtypeStruct((rows, width), f32),
        ),
        in_specs=[smem, smem, hbm, hbm, hbm],
        out_specs=(vmem, vmem, vmem),
        scratch_shapes=[
            own, own, pltpu.VMEM((1, rows), jnp.int32), pltpu.SemaphoreType.DMA((3,)),
            pltpu.VMEM((4 * rows, width), bf16),
            pltpu.VMEM((STEPS * rows, width), bf16),
            pltpu.VMEM((STEPS * rows, 4 * rows), bf16),
            pltpu.VMEM((4, 1, rows), jnp.int32),
            pltpu.VMEM((rows, 1), f32),
            pltpu.VMEM((rows, 1), f32),
            pltpu.VMEM((4, 1, rows), f32),
            pltpu.VMEM((3, 1, rows), f32),
            half, pltpu.VMEM((rows // 2, width), f32),
            half, half, half, half, half, half, half, half, half,
            own, own, own, own, own, own,
            pltpu.SemaphoreType.DMA((40,)),
            pltpu.SemaphoreType.DMA((40,)),
        ],
        compiler_params=pltpu.CompilerParams(
            collective_id=0, has_side_effects=True, vmem_limit_bytes=44 * MIB),
        cost_estimate=pl.CostEstimate(
            flops=2 * 3 * STEPS * rows * 4 * rows * width, bytes_accessed=12 * rows * width,
            transcendentals=2 * STEPS * rows * 4 * rows),
        name="contrast",
    )(log_scale, logit_bias, images, captions, labels.reshape(1, rows))
    return (loss.reshape(rows), image_grad, caption_grad)


def solution(mesh):
    in_specs = (P(("blk", "grp"), None), P(("blk", "grp"), None), P(("blk", "grp")), P(), P())
    out_specs = (P(("blk", "grp")), P(("blk", "grp"), None), P(("blk", "grp"), None))
    return jax.shard_map(body, mesh=mesh, in_specs=in_specs, out_specs=out_specs, check_vma=False)
```

```python
import jax
import jax.numpy as jnp
from jax import lax
from jax.experimental import pallas as pl
from jax.experimental.pallas import tpu as pltpu
from jax.sharding import PartitionSpec as P

STEPS = 3
ROW = 4
MIB = 2**20

epsilon = 1e-06

f32 = jnp.float32
bf16 = jnp.bfloat16


def places():
    blk_size = lax.axis_size("blk")
    half = blk_size // 2
    blk = lax.axis_index("blk")
    grp = lax.axis_index("grp")
    chip, core = grp // 2, grp % 2

    def along(start, steps):
        other = (start + steps + blk_size) % blk_size
        other_chip = (chip + start // half + other // half) % 2
        return (other, other_chip * 2 + core)

    def beside(start, steps):
        return start - start % ROW + (start + steps + ROW) % ROW

    def crosses(start, steps):
        return (start // half + (start + steps + blk_size) % blk_size // half) % 2

    def side(start, steps):
        change = crosses(start, 2 * steps)
        return (beside(start, -steps) + change * half) % blk_size, change

    def served(start, steps):
        other = beside(start, steps)
        change = crosses(other, 2 * steps)
        return (other + change * half) % blk_size, change

    def member(change):
        return (chip + change) % 2 * 2 + core

    left, left_change = side(blk, 1)
    right, right_change = side(blk, -1)
    from_right, from_right_change = served(blk, 1)
    from_left, from_left_change = served(blk, -1)
    targets = dict(
        core=(blk, chip * 2 + 1 - core),
        pair=(blk, (1 - chip) * 2 + core),
        cross=(blk, (1 - chip) * 2 + 1 - core),
        next=along(blk, 1),
        last=along(blk, -1),
        left=(left, member(left_change)),
        right=(right, member(right_change)),
        on=((from_right + 2) % blk_size, grp),
        home=((from_left - 2 + blk_size) % blk_size, grp),
    )
    sources = [targets[name] for name in ("core", "pair", "cross", "next", "last")]
    sources += [(from_right, member(from_right_change)), (from_left, member(from_left_change))]
    sources += [(side((blk - 2 + blk_size) % blk_size, 1)[0], grp), (side((blk + 2) % blk_size, -1)[0], grp)]
    return targets, sources


def kernel(log_scale_ref, bias_ref, img_hbm, cap_hbm, lab_hbm, loss_ref, dimg_ref, dcap_ref,
           img_ref, cap_ref, lab_ref, load_sems, imgs, caps, weights, labs, inv_img, inv_cap, loss_acc, loss_in, passing, own_terms,
           out_last, out_acc, out_far, acc_out, in_last, in_acc, in_passing, in_home, in_sum,
           core_out2, core_in2, core_out0, core_in0, pair_out, pair_in, send_sems, recv_sems):
    rows, width = dimg_ref.shape
    block_rows = 4 * rows
    piece, part = rows // 4, rows // 2
    place, sources = places()
    started = []

    def copy(source, target, to):
        index = len(started)
        made = pltpu.make_async_remote_copy(
            src_ref=source, dst_ref=target, send_sem=send_sems.at[index], recv_sem=recv_sems.at[index],
            device_id=place[to], device_id_type=pl.DeviceIdType.MESH)
        started.append(made)
        return made

    barrier = pltpu.get_barrier_semaphore()
    for to in sources:
        pl.semaphore_signal(barrier, inc=1, device_id=to, device_id_type=pl.DeviceIdType.MESH)

    loads = [pltpu.make_async_copy(source, target, load_sems.at[i])
             for i, (source, target) in enumerate(((img_hbm, img_ref), (cap_hbm, cap_ref), (lab_hbm, lab_ref)))]
    for made in loads:
        made.start()
    scale = jnp.exp(jnp.full((1, 1), log_scale_ref[0], f32))
    bias = bias_ref[0]

    def normalize(source, span, inverse_ref, target):
        wide = source[span, :].astype(f32)
        inverse = lax.rsqrt(jnp.sum(wide * wide, -1, keepdims=True) + epsilon)
        inverse_ref[span, :] = inverse
        target[span, :] = (wide * inverse).astype(bf16)

    loads[0].wait()
    for i in range(2):
        normalize(img_ref, pl.ds(i * part, part), inv_img, imgs)
    loads[1].wait()
    for i in range(2):
        normalize(cap_ref, pl.ds(i * part, part), inv_cap, caps)

    loads[2].wait()
    pl.semaphore_wait(barrier, len(place))

    def at(ref, start, index, size=piece):
        return ref.at[pl.ds(start + index * size, size)]

    lab_copies = [copy(lab_ref, labs.at[slot], to) for slot, to in ((1, "core"), (2, "pair"), (3, "cross"))]
    to_core = copy(at(imgs, 0, 0, rows), at(imgs, rows, 0, rows), "core")
    to_pair = [copy(at(imgs, 0, i), at(imgs, 2 * rows, i), "pair") for i in range(4)]
    pair_on = [copy(at(imgs, 2 * rows, i), at(imgs, 3 * rows, i), "core") for i in range(4)]
    to_next = [copy(at(caps, 0, i), at(caps, rows, i), "next") for i in range(4)]
    next_on = [copy(at(caps, rows, i), at(caps, 2 * rows, i), "next") for i in range(2)]
    to_left = [copy(at(caps, part, i), at(passing, 0, i), "left") for i in range(2)]
    left_on = [copy(at(passing, 0, i), at(caps, 2 * rows + part, i), "on") for i in range(2)]

    for made in lab_copies:
        made.start()
    to_core.start()
    for i in range(4):
        to_pair[i].start()
        to_next[i].start()
        if i < 2:
            to_left[i].start()
    labs[0] = lab_ref[...]

    row_index = lax.broadcasted_iota(jnp.int32, (rows, 1), 0) + (
        lax.axis_index("blk") * block_rows + lax.axis_index("grp") * rows)
    for slot in range(4):
        loss_acc[slot] = jnp.zeros((1, rows), f32)

    def score(start, size, slot):
        dots = lax.dot_general(caps[pl.ds(start, size), :], imgs[pl.ds(slot * rows, rows), :],
                               (((1,), (1,)), ((), ())), preferred_element_type=f32)
        logits = scale * dots + bias
        grown = jnp.exp(logits)
        total = 1.0 + grown
        inverse = 1.0 / total
        loss = jnp.log(total) + (grown - (total - 1.0)) * inverse
        weight = grown * inverse
        if start < rows:
            positive = labs[slot] == row_index[start:start + size]
            loss = loss - jnp.where(positive, logits, 0.0)
            weight = weight - jnp.where(positive, 1.0, 0.0)
        weights[pl.ds(start, size), pl.ds(slot * rows, rows)] = weight.astype(bf16)
        loss_acc[slot] = loss_acc[slot] + jnp.sum(loss, 0, keepdims=True)

    def caption_terms(start, size):
        return jnp.dot(weights[pl.ds(start, size), :], imgs[...], preferred_element_type=f32)

    def image_terms(slot, i):
        return lax.dot_general(weights[:, pl.ds(slot * rows + i * part, part)], caps[...],
                               (((0,), (0,)), ((), ())), preferred_element_type=f32)

    for made in lab_copies:
        made.wait_recv()
    score(0, rows, 0)
    to_core.wait_recv()
    for i in range(4):
        to_next[i].wait_recv()
        if i < 2:
            next_on[i].start()
            to_left[i].wait_recv()
            left_on[i].start()
        to_pair[i].wait_recv()
        pair_on[i].start()
        if i == 0:
            score(0, rows, 1)
        if i == 1:
            score(rows, part, 0)
            score(rows, part, 1)
        if i == 2:
            left_on[0].wait_recv()
            left_on[1].wait_recv()
            score(2 * rows + part, part, 0)
            score(2 * rows + part, part, 1)
    score(rows + part, part, 0)
    score(rows + part, part, 1)
    score(rows + part, part, 2)
    score(2 * rows + part, part, 2)
    for i in range(4):
        pair_on[i].wait_recv()
    score(rows + part, part, 3)

    out_last[...] = caption_terms(rows + part, part).astype(bf16)
    to_last = copy(out_last, in_last, "last")
    to_last.start()
    score(2 * rows + part, part, 3)
    out_far[...] = caption_terms(2 * rows + part, part).astype(bf16)
    to_right = [copy(at(out_far, 0, i), at(in_passing, 0, i), "right") for i in range(2)]
    right_on = [copy(at(in_passing, 0, i), at(in_home, 0, i), "home") for i in range(2)]
    for made in to_right:
        made.start()
    score(rows, part, 2)
    score(rows, part, 3)
    own_terms[...] = caption_terms(rows, part)
    back = [copy(at(out_acc, 0, i), at(in_acc, 0, i), "last") for i in range(2)]
    for i in range(2):
        next_on[i].wait_recv()
        start = 2 * rows + i * piece
        for slot in range(4):
            score(start, piece, slot)
        out_acc[pl.ds(i * piece, piece), :] = caption_terms(start, piece).astype(bf16)
        back[i].start()
        if i == 0:
            score(0, rows, 2)
            score(0, rows, 3)

    core2 = [copy(at(core_out2, 0, i, part), at(core_in2, 0, i, part), "core") for i in range(2)]
    pairs = [copy(at(pair_out, 0, i, part), at(pair_in, 0, i, part), "pair") for i in range(2)]
    core0 = [copy(at(core_out0, 0, i, part), at(core_in0, 0, i, part), "core") for i in range(2)]
    sums = [copy(at(acc_out, 0, i), at(in_sum, 0, i), "last") for i in range(2)]
    loss_copies = [copy(loss_acc.at[slot], loss_in.at[slot - 1], to)
                   for slot, to in ((1, "core"), (2, "pair"), (3, "cross"))]
    for i in range(2):
        core_out2[pl.ds(i * part, part), :] = image_terms(3, i).astype(bf16)
        core2[i].start()
        own = image_terms(2, i)
        core2[i].wait_recv()
        pair_out[pl.ds(i * part, part), :] = (own + core_in2[pl.ds(i * part, part), :].astype(f32)).astype(bf16)
        pairs[i].start()
        to_right[i].wait_recv()
        right_on[i].start()
    for made in loss_copies:
        made.start()
    for i in range(2):
        back[i].wait_recv()
        span = pl.ds(i * piece, piece)
        acc_out[span, :] = (own_terms[span, :] + in_acc[span, :].astype(f32)).astype(bf16)
        sums[i].start()
        core_out0[pl.ds(i * part, part), :] = image_terms(1, i).astype(bf16)
        core0[i].start()
    for i in range(2):
        dimg_ref[pl.ds(i * part, part), :] = image_terms(0, i)
    for i in range(2):
        dcap_ref[pl.ds(i * part, part), :] = caption_terms(i * part, part)
    for i in range(2):
        core0[i].wait_recv()
        span = pl.ds(i * part, part)
        dimg_ref[span, :] = dimg_ref[span, :] + core_in0[span, :].astype(f32)

    for made in loss_copies:
        made.wait_recv()
    loss_ref[...] = (loss_acc[0] + loss_in[0] + loss_in[1] + loss_in[2]) / (STEPS * block_rows)

    def unnormalize(source, span, inverse_ref, pull):
        inverse = inverse_ref[span, :]
        unit = source[span, :].astype(f32) * inverse
        pull = scale * pull
        return inverse * (pull - unit * jnp.sum(unit * pull, -1, keepdims=True))

    to_last.wait_recv()
    for i in range(2):
        right_on[i].wait_recv()
        span, near = pl.ds(part + i * piece, piece), pl.ds(i * piece, piece)
        pull = dcap_ref[span, :] + in_last[near, :].astype(f32) + in_home[near, :].astype(f32)
        dcap_ref[span, :] = unnormalize(cap_ref, span, inv_cap, pull)
    for i in range(2):
        sums[i].wait_recv()
        span = pl.ds(i * piece, piece)
        pull = dcap_ref[span, :] + in_sum[span, :].astype(f32)
        dcap_ref[span, :] = unnormalize(cap_ref, span, inv_cap, pull)
    for i in range(2):
        pairs[i].wait_recv()
        span = pl.ds(i * part, part)
        pull = dimg_ref[span, :] + pair_in[span, :].astype(f32)
        dimg_ref[span, :] = unnormalize(img_ref, span, inv_img, pull)
    for made in started:
        made.wait_send()


def store(loss_ref, dimg_ref, dcap_ref, loss_hbm, dimg_hbm, dcap_hbm, sems):
    pieces = []
    for source, target in ((dimg_ref, dimg_hbm), (dcap_ref, dcap_hbm)):
        size = source.shape[0] // 4
        pieces += [(source.at[pl.ds(i * size, size)], target.at[pl.ds(i * size, size)]) for i in range(4)]
    pieces.append((loss_ref, loss_hbm))
    copies = [pltpu.make_async_copy(source, target, sems.at[i]) for i, (source, target) in enumerate(pieces)]
    for made in copies:
        made.start()
    for made in copies:
        made.wait()


def body(images, captions, labels, log_scale, logit_bias):
    rows, width = images.shape
    vmem = pl.BlockSpec(memory_space=pltpu.VMEM)
    hbm = pl.BlockSpec(memory_space=pltpu.HBM)
    smem = pl.BlockSpec(memory_space=pltpu.SMEM)
    own = pltpu.VMEM((rows, width), bf16)
    half = pltpu.VMEM((rows // 2, width), bf16)
    loss, image_grad, caption_grad = pl.pallas_call(
        kernel,
        out_shape=(
            pltpu.VMEM((1, rows), f32),
            pltpu.VMEM((rows, width), f32),
            pltpu.VMEM((rows, width), f32),
        ),
        in_specs=[smem, smem, hbm, hbm, hbm],
        out_specs=(vmem, vmem, vmem),
        scratch_shapes=[
            own, own, pltpu.VMEM((1, rows), jnp.int32), pltpu.SemaphoreType.DMA((3,)),
            pltpu.VMEM((4 * rows, width), bf16),
            pltpu.VMEM((STEPS * rows, width), bf16),
            pltpu.VMEM((STEPS * rows, 4 * rows), bf16),
            pltpu.VMEM((4, 1, rows), jnp.int32),
            pltpu.VMEM((rows, 1), f32),
            pltpu.VMEM((rows, 1), f32),
            pltpu.VMEM((4, 1, rows), f32),
            pltpu.VMEM((3, 1, rows), f32),
            half, pltpu.VMEM((rows // 2, width), f32),
            half, half, half, half, half, half, half, half, half,
            own, own, own, own, own, own,
            pltpu.SemaphoreType.DMA((40,)),
            pltpu.SemaphoreType.DMA((40,)),
        ],
        compiler_params=pltpu.CompilerParams(
            collective_id=0, has_side_effects=True, vmem_limit_bytes=44 * MIB),
        cost_estimate=pl.CostEstimate(
            flops=2 * 3 * STEPS * rows * 4 * rows * width, bytes_accessed=12 * rows * width,
            transcendentals=2 * STEPS * rows * 4 * rows),
        name="contrast",
    )(log_scale, logit_bias, *(pltpu.with_memory_space_constraint(value, pltpu.HBM)
                               for value in (images, captions, labels.reshape(1, rows))))
    loss, image_grad, caption_grad = pl.pallas_call(
        store,
        out_shape=(
            jax.ShapeDtypeStruct((1, rows), f32),
            jax.ShapeDtypeStruct((rows, width), f32),
            jax.ShapeDtypeStruct((rows, width), f32),
        ),
        in_specs=[vmem, vmem, vmem],
        out_specs=(hbm, hbm, hbm),
        scratch_shapes=[pltpu.SemaphoreType.DMA((9,))],
        compiler_params=pltpu.CompilerParams(vmem_limit_bytes=4 * MIB),
        name="store",
    )(loss, image_grad, caption_grad)
    return (loss.reshape(rows), image_grad, caption_grad)


def solution(mesh):
    in_specs = (P(("blk", "grp"), None), P(("blk", "grp"), None), P(("blk", "grp")), P(), P())
    out_specs = (P(("blk", "grp")), P(("blk", "grp"), None), P(("blk", "grp"), None))
    return jax.shard_map(body, mesh=mesh, in_specs=in_specs, out_specs=out_specs, check_vma=False)
```

```python
import jax
import jax.numpy as jnp
from jax import lax
from jax.experimental import pallas as pl
from jax.experimental.pallas import tpu as pltpu
from jax.sharding import PartitionSpec as P

STEPS = 3
ROW = 4
MIB = 2**20

epsilon = 1e-06

f32 = jnp.float32
bf16 = jnp.bfloat16


def places():
    blk_size = lax.axis_size("blk")
    half = blk_size // 2
    blk = lax.axis_index("blk")
    grp = lax.axis_index("grp")
    chip, core = grp // 2, grp % 2

    def along(start, steps):
        other = (start + steps + blk_size) % blk_size
        other_chip = (chip + start // half + other // half) % 2
        return (other, other_chip * 2 + core)

    def beside(start, steps):
        return start - start % ROW + (start + steps + ROW) % ROW

    def crosses(start, steps):
        return (start // half + (start + steps + blk_size) % blk_size // half) % 2

    def side(start, steps):
        change = crosses(start, 2 * steps)
        return (beside(start, -steps) + change * half) % blk_size, change

    def served(start, steps):
        other = beside(start, steps)
        change = crosses(other, 2 * steps)
        return (other + change * half) % blk_size, change

    def member(change):
        return (chip + change) % 2 * 2 + core

    left, left_change = side(blk, 1)
    right, right_change = side(blk, -1)
    from_right, from_right_change = served(blk, 1)
    from_left, from_left_change = served(blk, -1)
    targets = dict(
        core=(blk, chip * 2 + 1 - core),
        pair=(blk, (1 - chip) * 2 + core),
        cross=(blk, (1 - chip) * 2 + 1 - core),
        next=along(blk, 1),
        last=along(blk, -1),
        left=(left, member(left_change)),
        right=(right, member(right_change)),
        on=((from_right + 2) % blk_size, grp),
        home=((from_left - 2 + blk_size) % blk_size, grp),
    )
    sources = [targets[name] for name in ("core", "pair", "cross", "next", "last")]
    sources += [(from_right, member(from_right_change)), (from_left, member(from_left_change))]
    sources += [(side((blk - 2 + blk_size) % blk_size, 1)[0], grp), (side((blk + 2) % blk_size, -1)[0], grp)]
    return targets, sources


def kernel(log_scale_ref, bias_ref, img_hbm, cap_hbm, lab_hbm, loss_ref, dimg_ref, dcap_ref,
           img_ref, cap_ref, lab_ref, load_sems, imgs, caps, weights, labs, inv_img, inv_cap, loss_acc, loss_in, passing, own_terms,
           out_last, out_acc, out_far, acc_out, in_last, in_acc, in_passing, in_home, in_sum,
           core_out2, core_in2, core_out0, core_in0, pair_out, pair_in, send_sems, recv_sems):
    rows, width = dimg_ref.shape
    block_rows = 4 * rows
    piece, part = rows // 4, rows // 2
    place, sources = places()
    started = []

    def copy(source, target, to):
        index = len(started)
        made = pltpu.make_async_remote_copy(
            src_ref=source, dst_ref=target, send_sem=send_sems.at[index], recv_sem=recv_sems.at[index],
            device_id=place[to], device_id_type=pl.DeviceIdType.MESH)
        started.append(made)
        return made

    barrier = pltpu.get_barrier_semaphore()
    for to in sources:
        pl.semaphore_signal(barrier, inc=1, device_id=to, device_id_type=pl.DeviceIdType.MESH)

    loads = [pltpu.make_async_copy(source, target, load_sems.at[i])
             for i, (source, target) in enumerate(((img_hbm, img_ref), (cap_hbm, cap_ref), (lab_hbm, lab_ref)))]
    for made in loads:
        made.start()
    scale = jnp.exp(jnp.full((1, 1), log_scale_ref[0], f32))
    bias = bias_ref[0]

    def normalize(source, span, inverse_ref, target):
        wide = source[span, :].astype(f32)
        inverse = lax.rsqrt(jnp.sum(wide * wide, -1, keepdims=True) + epsilon)
        inverse_ref[span, :] = inverse
        target[span, :] = (wide * inverse).astype(bf16)

    loads[0].wait()
    for i in range(2):
        normalize(img_ref, pl.ds(i * part, part), inv_img, imgs)
    loads[1].wait()
    for i in range(2):
        normalize(cap_ref, pl.ds(i * part, part), inv_cap, caps)

    loads[2].wait()
    pl.semaphore_wait(barrier, len(place))

    def at(ref, start, index, size=piece):
        return ref.at[pl.ds(start + index * size, size)]

    lab_copies = [copy(lab_ref, labs.at[slot], to) for slot, to in ((1, "core"), (2, "pair"), (3, "cross"))]
    to_core = copy(at(imgs, 0, 0, rows), at(imgs, rows, 0, rows), "core")
    to_pair = [copy(at(imgs, 0, i), at(imgs, 2 * rows, i), "pair") for i in range(4)]
    pair_on = [copy(at(imgs, 2 * rows, i), at(imgs, 3 * rows, i), "core") for i in range(4)]
    to_next = [copy(at(caps, 0, i), at(caps, rows, i), "next") for i in range(4)]
    next_on = [copy(at(caps, rows, i), at(caps, 2 * rows, i), "next") for i in range(2)]
    to_left = [copy(at(caps, part, i), at(passing, 0, i), "left") for i in range(2)]
    left_on = [copy(at(passing, 0, i), at(caps, 2 * rows + part, i), "on") for i in range(2)]

    for made in lab_copies:
        made.start()
    to_core.start()
    for i in range(4):
        to_pair[i].start()
        to_next[i].start()
        if i < 2:
            to_left[i].start()
    labs[0] = lab_ref[...]

    row_index = lax.broadcasted_iota(jnp.int32, (rows, 1), 0) + (
        lax.axis_index("blk") * block_rows + lax.axis_index("grp") * rows)
    for slot in range(4):
        loss_acc[slot] = jnp.zeros((1, rows), f32)

    def score(start, size, slot):
        dots = lax.dot_general(caps[pl.ds(start, size), :], imgs[pl.ds(slot * rows, rows), :],
                               (((1,), (1,)), ((), ())), preferred_element_type=f32)
        logits = scale * dots + bias
        grown = jnp.exp(logits)
        total = 1.0 + grown
        inverse = 1.0 / total
        loss = jnp.log(total) + (grown - (total - 1.0)) * inverse
        weight = grown * inverse
        if start < rows:
            positive = labs[slot] == row_index[start:start + size]
            loss = loss - jnp.where(positive, logits, 0.0)
            weight = weight - jnp.where(positive, 1.0, 0.0)
        weights[pl.ds(start, size), pl.ds(slot * rows, rows)] = weight.astype(bf16)
        loss_acc[slot] = loss_acc[slot] + jnp.sum(loss, 0, keepdims=True)

    def caption_terms(start, size):
        return jnp.dot(weights[pl.ds(start, size), :], imgs[...], preferred_element_type=f32)

    def image_terms(slot, i):
        return lax.dot_general(weights[:, pl.ds(slot * rows + i * part, part)], caps[...],
                               (((0,), (0,)), ((), ())), preferred_element_type=f32)

    for made in lab_copies:
        made.wait_recv()
    score(0, rows, 0)
    to_core.wait_recv()
    for i in range(4):
        to_pair[i].wait_recv()
        pair_on[i].start()
        if i < 2:
            to_left[i].wait_recv()
            left_on[i].start()
        to_next[i].wait_recv()
        if i < 2:
            next_on[i].start()
        if i == 0:
            score(0, rows, 1)
        if i == 1:
            score(rows, part, 0)
            score(rows, part, 1)
        if i == 2:
            left_on[0].wait_recv()
            left_on[1].wait_recv()
            score(2 * rows + part, part, 0)
            score(2 * rows + part, part, 1)
    score(rows + part, part, 0)
    score(rows + part, part, 1)
    score(rows + part, part, 2)
    score(2 * rows + part, part, 2)
    score(rows, part, 2)
    score(0, rows, 2)
    for i in range(4):
        pair_on[i].wait_recv()
    score(rows + part, part, 3)

    out_last[...] = caption_terms(rows + part, part).astype(bf16)
    to_last = copy(out_last, in_last, "last")
    to_last.start()
    score(2 * rows + part, part, 3)
    out_far[...] = caption_terms(2 * rows + part, part).astype(bf16)
    to_right = [copy(at(out_far, 0, i), at(in_passing, 0, i), "right") for i in range(2)]
    right_on = [copy(at(in_passing, 0, i), at(in_home, 0, i), "home") for i in range(2)]
    for made in to_right:
        made.start()
    score(rows, part, 3)
    score(0, rows, 3)
    back = [copy(at(out_acc, 0, i), at(in_acc, 0, i), "last") for i in range(2)]
    for i in range(2):
        next_on[i].wait_recv()
        start = 2 * rows + i * piece
        for slot in range(4):
            score(start, piece, slot)
        if i == 0:
            out_acc[pl.ds(0, piece), :] = caption_terms(start, piece).astype(bf16)
            back[0].start()

    core2 = [copy(at(core_out2, 0, i, part), at(core_in2, 0, i, part), "core") for i in range(2)]
    pairs = [copy(at(pair_out, 0, i, part), at(pair_in, 0, i, part), "pair") for i in range(2)]
    core0 = [copy(at(core_out0, 0, i, part), at(core_in0, 0, i, part), "core") for i in range(2)]
    sums = [copy(at(acc_out, 0, i), at(in_sum, 0, i), "last") for i in range(2)]
    loss_copies = [copy(loss_acc.at[slot], loss_in.at[slot - 1], to)
                   for slot, to in ((1, "core"), (2, "pair"), (3, "cross"))]
    for i in range(2):
        core_out2[pl.ds(i * part, part), :] = image_terms(3, i).astype(bf16)
        core2[i].start()
        if i == 0:
            out_acc[pl.ds(piece, piece), :] = caption_terms(2 * rows + piece, piece).astype(bf16)
            back[1].start()
        own = image_terms(2, i)
        core2[i].wait_recv()
        pair_out[pl.ds(i * part, part), :] = (own + core_in2[pl.ds(i * part, part), :].astype(f32)).astype(bf16)
        pairs[i].start()
        to_right[i].wait_recv()
        right_on[i].start()
    own_terms[...] = caption_terms(rows, part)
    for made in loss_copies:
        made.start()
    for i in range(2):
        back[i].wait_recv()
        span = pl.ds(i * piece, piece)
        acc_out[span, :] = (own_terms[span, :] + in_acc[span, :].astype(f32)).astype(bf16)
        sums[i].start()
        core_out0[pl.ds(i * part, part), :] = image_terms(1, i).astype(bf16)
        core0[i].start()
    for i in range(2):
        dimg_ref[pl.ds(i * part, part), :] = image_terms(0, i)
    for i in range(2):
        dcap_ref[pl.ds(i * part, part), :] = caption_terms(i * part, part)
    for i in range(2):
        core0[i].wait_recv()
        span = pl.ds(i * part, part)
        dimg_ref[span, :] = dimg_ref[span, :] + core_in0[span, :].astype(f32)

    for made in loss_copies:
        made.wait_recv()
    loss_ref[...] = (loss_acc[0] + loss_in[0] + loss_in[1] + loss_in[2]) / (STEPS * block_rows)

    def unnormalize(source, span, inverse_ref, pull):
        inverse = inverse_ref[span, :]
        unit = source[span, :].astype(f32) * inverse
        pull = scale * pull
        return inverse * (pull - unit * jnp.sum(unit * pull, -1, keepdims=True))

    to_last.wait_recv()
    for i in range(2):
        right_on[i].wait_recv()
        span, near = pl.ds(part + i * piece, piece), pl.ds(i * piece, piece)
        pull = dcap_ref[span, :] + in_last[near, :].astype(f32) + in_home[near, :].astype(f32)
        dcap_ref[span, :] = unnormalize(cap_ref, span, inv_cap, pull)
    for i in range(2):
        sums[i].wait_recv()
        span = pl.ds(i * piece, piece)
        pull = dcap_ref[span, :] + in_sum[span, :].astype(f32)
        dcap_ref[span, :] = unnormalize(cap_ref, span, inv_cap, pull)
    for i in range(2):
        pairs[i].wait_recv()
        span = pl.ds(i * part, part)
        pull = dimg_ref[span, :] + pair_in[span, :].astype(f32)
        dimg_ref[span, :] = unnormalize(img_ref, span, inv_img, pull)
    for made in started:
        made.wait_send()


def store(loss_ref, dimg_ref, dcap_ref, loss_hbm, dimg_hbm, dcap_hbm, sems):
    pieces = []
    for source, target in ((dimg_ref, dimg_hbm), (dcap_ref, dcap_hbm)):
        size = source.shape[0] // 4
        pieces += [(source.at[pl.ds(i * size, size)], target.at[pl.ds(i * size, size)]) for i in range(4)]
    pieces.append((loss_ref, loss_hbm))
    copies = [pltpu.make_async_copy(source, target, sems.at[i]) for i, (source, target) in enumerate(pieces)]
    for made in copies:
        made.start()
    for made in copies:
        made.wait()


def body(images, captions, labels, log_scale, logit_bias):
    rows, width = images.shape
    vmem = pl.BlockSpec(memory_space=pltpu.VMEM)
    hbm = pl.BlockSpec(memory_space=pltpu.HBM)
    smem = pl.BlockSpec(memory_space=pltpu.SMEM)
    own = pltpu.VMEM((rows, width), bf16)
    half = pltpu.VMEM((rows // 2, width), bf16)
    loss, image_grad, caption_grad = pl.pallas_call(
        kernel,
        out_shape=(
            pltpu.VMEM((1, rows), f32),
            pltpu.VMEM((rows, width), f32),
            pltpu.VMEM((rows, width), f32),
        ),
        in_specs=[smem, smem, hbm, hbm, hbm],
        out_specs=(vmem, vmem, vmem),
        scratch_shapes=[
            own, own, pltpu.VMEM((1, rows), jnp.int32), pltpu.SemaphoreType.DMA((3,)),
            pltpu.VMEM((4 * rows, width), bf16),
            pltpu.VMEM((STEPS * rows, width), bf16),
            pltpu.VMEM((STEPS * rows, 4 * rows), bf16),
            pltpu.VMEM((4, 1, rows), jnp.int32),
            pltpu.VMEM((rows, 1), f32),
            pltpu.VMEM((rows, 1), f32),
            pltpu.VMEM((4, 1, rows), f32),
            pltpu.VMEM((3, 1, rows), f32),
            half, pltpu.VMEM((rows // 2, width), f32),
            half, half, half, half, half, half, half, half, half,
            own, own, own, own, own, own,
            pltpu.SemaphoreType.DMA((40,)),
            pltpu.SemaphoreType.DMA((40,)),
        ],
        compiler_params=pltpu.CompilerParams(
            collective_id=0, has_side_effects=True, vmem_limit_bytes=44 * MIB),
        cost_estimate=pl.CostEstimate(
            flops=2 * 3 * STEPS * rows * 4 * rows * width, bytes_accessed=12 * rows * width,
            transcendentals=2 * STEPS * rows * 4 * rows),
        name="contrast",
    )(log_scale, logit_bias, *(pltpu.with_memory_space_constraint(value, pltpu.HBM)
                               for value in (images, captions, labels.reshape(1, rows))))
    loss, image_grad, caption_grad = pl.pallas_call(
        store,
        out_shape=(
            jax.ShapeDtypeStruct((1, rows), f32),
            jax.ShapeDtypeStruct((rows, width), f32),
            jax.ShapeDtypeStruct((rows, width), f32),
        ),
        in_specs=[vmem, vmem, vmem],
        out_specs=(hbm, hbm, hbm),
        scratch_shapes=[pltpu.SemaphoreType.DMA((9,))],
        compiler_params=pltpu.CompilerParams(vmem_limit_bytes=4 * MIB),
        name="store",
    )(loss, image_grad, caption_grad)
    return (loss.reshape(rows), image_grad, caption_grad)


def solution(mesh):
    in_specs = (P(("blk", "grp"), None), P(("blk", "grp"), None), P(("blk", "grp")), P(), P())
    out_specs = (P(("blk", "grp")), P(("blk", "grp"), None), P(("blk", "grp"), None))
    return jax.shard_map(body, mesh=mesh, in_specs=in_specs, out_specs=out_specs, check_vma=False)
```

```python
import jax
import jax.numpy as jnp
from jax import lax
from jax.experimental import pallas as pl
from jax.experimental.pallas import tpu as pltpu
from jax.sharding import PartitionSpec as P

STEPS = 3
ROW = 4
MIB = 2**20

epsilon = 1e-06

f32 = jnp.float32
bf16 = jnp.bfloat16


def places():
    blk_size = lax.axis_size("blk")
    half = blk_size // 2
    blk = lax.axis_index("blk")
    grp = lax.axis_index("grp")
    chip, core = grp // 2, grp % 2

    def along(start, steps):
        other = (start + steps + blk_size) % blk_size
        other_chip = (chip + start // half + other // half) % 2
        return (other, other_chip * 2 + core)

    def beside(start, steps):
        return start - start % ROW + (start + steps + ROW) % ROW

    def crosses(start, steps):
        return (start // half + (start + steps + blk_size) % blk_size // half) % 2

    def side(start, steps):
        change = crosses(start, 2 * steps)
        return (beside(start, -steps) + change * half) % blk_size, change

    def served(start, steps):
        other = beside(start, steps)
        change = crosses(other, 2 * steps)
        return (other + change * half) % blk_size, change

    def member(change):
        return (chip + change) % 2 * 2 + core

    left, left_change = side(blk, 1)
    right, right_change = side(blk, -1)
    from_right, from_right_change = served(blk, 1)
    from_left, from_left_change = served(blk, -1)
    targets = dict(
        core=(blk, chip * 2 + 1 - core),
        pair=(blk, (1 - chip) * 2 + core),
        cross=(blk, (1 - chip) * 2 + 1 - core),
        next=along(blk, 1),
        last=along(blk, -1),
        left=(left, member(left_change)),
        right=(right, member(right_change)),
        on=((from_right + 2) % blk_size, grp),
        home=((from_left - 2 + blk_size) % blk_size, grp),
    )
    sources = [targets[name] for name in ("core", "pair", "cross", "next", "last")]
    sources += [(from_right, member(from_right_change)), (from_left, member(from_left_change))]
    sources += [(side((blk - 2 + blk_size) % blk_size, 1)[0], grp), (side((blk + 2) % blk_size, -1)[0], grp)]
    return targets, sources


def kernel(log_scale_ref, bias_ref, img_hbm, cap_hbm, lab_hbm, loss_ref, dimg_ref, dcap_ref,
           img_ref, cap_ref, lab_ref, load_sems, imgs, caps, weights, labs, inv_img, inv_cap, loss_acc, loss_in, passing, own_terms,
           out_last, out_acc, out_far, acc_out, in_last, in_acc, in_passing, in_home, in_sum,
           core_out2, core_in2, core_out0, core_in0, pair_out, pair_in, send_sems, recv_sems):
    rows, width = dimg_ref.shape
    block_rows = 4 * rows
    piece, part = rows // 4, rows // 2
    place, sources = places()
    started = []

    def copy(source, target, to):
        index = len(started)
        made = pltpu.make_async_remote_copy(
            src_ref=source, dst_ref=target, send_sem=send_sems.at[index], recv_sem=recv_sems.at[index],
            device_id=place[to], device_id_type=pl.DeviceIdType.MESH)
        started.append(made)
        return made

    barrier = pltpu.get_barrier_semaphore()
    for to in sources:
        pl.semaphore_signal(barrier, inc=1, device_id=to, device_id_type=pl.DeviceIdType.MESH)

    loads = [pltpu.make_async_copy(source, target, load_sems.at[i])
             for i, (source, target) in enumerate(((img_hbm, img_ref), (cap_hbm, cap_ref), (lab_hbm, lab_ref)))]
    for made in loads:
        made.start()
    scale = jnp.exp(jnp.full((1, 1), log_scale_ref[0], f32))
    bias = bias_ref[0]

    def normalize(source, span, inverse_ref, target):
        wide = source[span, :].astype(f32)
        inverse = lax.rsqrt(jnp.sum(wide * wide, -1, keepdims=True) + epsilon)
        inverse_ref[span, :] = inverse
        target[span, :] = (wide * inverse).astype(bf16)

    loads[0].wait()
    for i in range(2):
        normalize(img_ref, pl.ds(i * part, part), inv_img, imgs)
    loads[1].wait()
    for i in range(2):
        normalize(cap_ref, pl.ds(i * part, part), inv_cap, caps)

    loads[2].wait()
    pl.semaphore_wait(barrier, len(place))

    def at(ref, start, index, size=piece):
        return ref.at[pl.ds(start + index * size, size)]

    lab_copies = [copy(lab_ref, labs.at[slot], to) for slot, to in ((1, "core"), (2, "pair"), (3, "cross"))]
    to_core = copy(at(imgs, 0, 0, rows), at(imgs, rows, 0, rows), "core")
    to_pair = [copy(at(imgs, 0, i), at(imgs, 2 * rows, i), "pair") for i in range(4)]
    pair_on = [copy(at(imgs, 2 * rows, i), at(imgs, 3 * rows, i), "core") for i in range(4)]
    to_next = [copy(at(caps, 0, i), at(caps, rows, i), "next") for i in range(4)]
    next_on = [copy(at(caps, rows, i), at(caps, 2 * rows, i), "next") for i in range(2)]
    to_left = [copy(at(caps, part, i), at(passing, 0, i), "left") for i in range(2)]
    left_on = [copy(at(passing, 0, i), at(caps, 2 * rows + part, i), "on") for i in range(2)]

    for i in range(4):
        to_next[i].start()
        if i < 2:
            to_left[i].start()
        to_pair[i].start()
        if i == 0:
            to_core.start()
            for made in lab_copies:
                made.start()
    labs[0] = lab_ref[...]

    row_index = lax.broadcasted_iota(jnp.int32, (rows, 1), 0) + (
        lax.axis_index("blk") * block_rows + lax.axis_index("grp") * rows)
    for slot in range(4):
        loss_acc[slot] = jnp.zeros((1, rows), f32)

    def score(start, size, slot):
        dots = lax.dot_general(caps[pl.ds(start, size), :], imgs[pl.ds(slot * rows, rows), :],
                               (((1,), (1,)), ((), ())), preferred_element_type=f32)
        logits = scale * dots + bias
        grown = jnp.exp(logits)
        total = 1.0 + grown
        inverse = 1.0 / total
        loss = jnp.log(total) + (grown - (total - 1.0)) * inverse
        weight = grown * inverse
        if start < rows:
            positive = labs[slot] == row_index[start:start + size]
            loss = loss - jnp.where(positive, logits, 0.0)
            weight = weight - jnp.where(positive, 1.0, 0.0)
        weights[pl.ds(start, size), pl.ds(slot * rows, rows)] = weight.astype(bf16)
        loss_acc[slot] = loss_acc[slot] + jnp.sum(loss, 0, keepdims=True)

    def caption_terms(start, size):
        return jnp.dot(weights[pl.ds(start, size), :], imgs[...], preferred_element_type=f32)

    def image_terms(slot, i):
        return lax.dot_general(weights[:, pl.ds(slot * rows + i * part, part)], caps[...],
                               (((0,), (0,)), ((), ())), preferred_element_type=f32)

    for made in lab_copies:
        made.wait_recv()
    score(0, rows, 0)
    to_core.wait_recv()
    for i in range(4):
        to_pair[i].wait_recv()
        pair_on[i].start()
        if i < 2:
            to_left[i].wait_recv()
            left_on[i].start()
        to_next[i].wait_recv()
        if i < 2:
            next_on[i].start()
        if i == 0:
            score(0, rows, 1)
        if i == 1:
            score(rows, part, 0)
            score(rows, part, 1)
        if i == 2:
            left_on[0].wait_recv()
            left_on[1].wait_recv()
            score(2 * rows + part, part, 0)
            score(2 * rows + part, part, 1)
    score(rows + part, part, 0)
    score(rows + part, part, 1)
    score(rows + part, part, 2)
    score(2 * rows + part, part, 2)
    score(rows, part, 2)
    score(0, rows, 2)
    for i in range(4):
        pair_on[i].wait_recv()
    score(rows + part, part, 3)

    out_last[...] = caption_terms(rows + part, part).astype(bf16)
    to_last = copy(out_last, in_last, "last")
    to_last.start()
    score(2 * rows + part, part, 3)
    out_far[...] = caption_terms(2 * rows + part, part).astype(bf16)
    to_right = [copy(at(out_far, 0, i), at(in_passing, 0, i), "right") for i in range(2)]
    right_on = [copy(at(in_passing, 0, i), at(in_home, 0, i), "home") for i in range(2)]
    for made in to_right:
        made.start()
    score(rows, part, 3)
    score(0, rows, 3)
    back = [copy(at(out_acc, 0, i), at(in_acc, 0, i), "last") for i in range(2)]
    for i in range(2):
        next_on[i].wait_recv()
        start = 2 * rows + i * piece
        for slot in range(4):
            score(start, piece, slot)
        if i == 0:
            out_acc[pl.ds(0, piece), :] = caption_terms(start, piece).astype(bf16)
            back[0].start()

    core2 = [copy(at(core_out2, 0, i, part), at(core_in2, 0, i, part), "core") for i in range(2)]
    pairs = [copy(at(pair_out, 0, i, part), at(pair_in, 0, i, part), "pair") for i in range(2)]
    core0 = [copy(at(core_out0, 0, i, part), at(core_in0, 0, i, part), "core") for i in range(2)]
    sums = [copy(at(acc_out, 0, i), at(in_sum, 0, i), "last") for i in range(2)]
    loss_copies = [copy(loss_acc.at[slot], loss_in.at[slot - 1], to)
                   for slot, to in ((1, "core"), (2, "pair"), (3, "cross"))]
    for i in range(2):
        core_out2[pl.ds(i * part, part), :] = image_terms(3, i).astype(bf16)
        core2[i].start()
        own = image_terms(2, i)
        if i == 0:
            out_acc[pl.ds(piece, piece), :] = caption_terms(2 * rows + piece, piece).astype(bf16)
            back[1].start()
        core2[i].wait_recv()
        pair_out[pl.ds(i * part, part), :] = (own + core_in2[pl.ds(i * part, part), :].astype(f32)).astype(bf16)
        pairs[i].start()
        to_right[i].wait_recv()
        right_on[i].start()
    own_terms[...] = caption_terms(rows, part)
    for made in loss_copies:
        made.start()
    for i in range(2):
        back[i].wait_recv()
        span = pl.ds(i * piece, piece)
        acc_out[span, :] = (own_terms[span, :] + in_acc[span, :].astype(f32)).astype(bf16)
        sums[i].start()
        core_out0[pl.ds(i * part, part), :] = image_terms(1, i).astype(bf16)
        core0[i].start()
    for i in range(2):
        dimg_ref[pl.ds(i * part, part), :] = image_terms(0, i)
    for i in range(2):
        dcap_ref[pl.ds(i * part, part), :] = caption_terms(i * part, part)
    for i in range(2):
        core0[i].wait_recv()
        span = pl.ds(i * part, part)
        dimg_ref[span, :] = dimg_ref[span, :] + core_in0[span, :].astype(f32)

    for made in loss_copies:
        made.wait_recv()
    loss_ref[...] = (loss_acc[0] + loss_in[0] + loss_in[1] + loss_in[2]) / (STEPS * block_rows)

    def unnormalize(source, span, inverse_ref, pull):
        inverse = inverse_ref[span, :]
        unit = source[span, :].astype(f32) * inverse
        pull = scale * pull
        return inverse * (pull - unit * jnp.sum(unit * pull, -1, keepdims=True))

    to_last.wait_recv()
    for i in range(2):
        right_on[i].wait_recv()
        span, near = pl.ds(part + i * piece, piece), pl.ds(i * piece, piece)
        pull = dcap_ref[span, :] + in_last[near, :].astype(f32) + in_home[near, :].astype(f32)
        dcap_ref[span, :] = unnormalize(cap_ref, span, inv_cap, pull)
    for i in range(2):
        sums[i].wait_recv()
        span = pl.ds(i * piece, piece)
        pull = dcap_ref[span, :] + in_sum[span, :].astype(f32)
        dcap_ref[span, :] = unnormalize(cap_ref, span, inv_cap, pull)
    for i in range(2):
        pairs[i].wait_recv()
        span = pl.ds(i * part, part)
        pull = dimg_ref[span, :] + pair_in[span, :].astype(f32)
        dimg_ref[span, :] = unnormalize(img_ref, span, inv_img, pull)
    for made in started:
        made.wait_send()


def store(loss_ref, dimg_ref, dcap_ref, loss_hbm, dimg_hbm, dcap_hbm, sems):
    pieces = []
    for source, target in ((dimg_ref, dimg_hbm), (dcap_ref, dcap_hbm)):
        size = source.shape[0] // 4
        pieces += [(source.at[pl.ds(i * size, size)], target.at[pl.ds(i * size, size)]) for i in range(4)]
    pieces.append((loss_ref, loss_hbm))
    copies = [pltpu.make_async_copy(source, target, sems.at[i]) for i, (source, target) in enumerate(pieces)]
    for made in copies:
        made.start()
    for made in copies:
        made.wait()


def body(images, captions, labels, log_scale, logit_bias):
    rows, width = images.shape
    vmem = pl.BlockSpec(memory_space=pltpu.VMEM)
    hbm = pl.BlockSpec(memory_space=pltpu.HBM)
    smem = pl.BlockSpec(memory_space=pltpu.SMEM)
    own = pltpu.VMEM((rows, width), bf16)
    half = pltpu.VMEM((rows // 2, width), bf16)
    loss, image_grad, caption_grad = pl.pallas_call(
        kernel,
        out_shape=(
            pltpu.VMEM((1, rows), f32),
            pltpu.VMEM((rows, width), f32),
            pltpu.VMEM((rows, width), f32),
        ),
        in_specs=[smem, smem, hbm, hbm, hbm],
        out_specs=(vmem, vmem, vmem),
        scratch_shapes=[
            own, own, pltpu.VMEM((1, rows), jnp.int32), pltpu.SemaphoreType.DMA((3,)),
            pltpu.VMEM((4 * rows, width), bf16),
            pltpu.VMEM((STEPS * rows, width), bf16),
            pltpu.VMEM((STEPS * rows, 4 * rows), bf16),
            pltpu.VMEM((4, 1, rows), jnp.int32),
            pltpu.VMEM((rows, 1), f32),
            pltpu.VMEM((rows, 1), f32),
            pltpu.VMEM((4, 1, rows), f32),
            pltpu.VMEM((3, 1, rows), f32),
            half, pltpu.VMEM((rows // 2, width), f32),
            half, half, half, half, half, half, half, half, half,
            own, own, own, own, own, own,
            pltpu.SemaphoreType.DMA((40,)),
            pltpu.SemaphoreType.DMA((40,)),
        ],
        compiler_params=pltpu.CompilerParams(
            collective_id=0, has_side_effects=True, vmem_limit_bytes=44 * MIB),
        cost_estimate=pl.CostEstimate(
            flops=2 * 3 * STEPS * rows * 4 * rows * width, bytes_accessed=12 * rows * width,
            transcendentals=2 * STEPS * rows * 4 * rows),
        name="contrast",
    )(log_scale, logit_bias, *(pltpu.with_memory_space_constraint(value, pltpu.HBM)
                               for value in (images, captions, labels.reshape(1, rows))))
    loss, image_grad, caption_grad = pl.pallas_call(
        store,
        out_shape=(
            jax.ShapeDtypeStruct((1, rows), f32),
            jax.ShapeDtypeStruct((rows, width), f32),
            jax.ShapeDtypeStruct((rows, width), f32),
        ),
        in_specs=[vmem, vmem, vmem],
        out_specs=(hbm, hbm, hbm),
        scratch_shapes=[pltpu.SemaphoreType.DMA((9,))],
        compiler_params=pltpu.CompilerParams(vmem_limit_bytes=4 * MIB),
        name="store",
    )(loss, image_grad, caption_grad)
    return (loss.reshape(rows), image_grad, caption_grad)


def solution(mesh):
    in_specs = (P(("blk", "grp"), None), P(("blk", "grp"), None), P(("blk", "grp")), P(), P())
    out_specs = (P(("blk", "grp")), P(("blk", "grp"), None), P(("blk", "grp"), None))
    return jax.shard_map(body, mesh=mesh, in_specs=in_specs, out_specs=out_specs, check_vma=False)
```
